32 devices in a mesh: grp: 4 (over y, core), seq: 8 (over z, x).
Axes of the slice: x: 2, y: 2, z: 4, core: 2. Of those that a mesh axis runs over, the one named last changes fastest.
Arguments:
- queries: bfloat16 [4096, 8192], P(('grp', 'seq')), may hold values from -8 to 8
- image_keys: bfloat16 [2048, 1024], P('grp'), may hold values from -8 to 8
- image_values: bfloat16 [2048, 1024], P('grp'), may hold values from -12 to 12
- gate_logit: float32 [1], replicated, may hold values from 0.5 to 1.5
- block_image: int32 [32, 1], P('grp'), may hold values from 0 to 3
- image_counts: int32 [4], replicated, may hold values from 128 to 512, as said below
- output_grad: bfloat16 [4096, 8192], P(('grp', 'seq')), may hold values from -6 to 6
Outputs:
- attended: bfloat16 [4096, 8192], P(('grp', 'seq'))
- query_grad: bfloat16 [4096, 8192], P(('grp', 'seq'))
- key_grad: bfloat16 [2048, 1024], P(('grp', 'seq'))
- value_grad: bfloat16 [2048, 1024], P(('grp', 'seq'))
The draws below stay inside these ranges and needn't reach their ends.
Inputs may be any that keep to these rules, and one draw needn't show every extreme that they name: `block_image`: block b covers text rows b * 128 to (b + 1) * 128 - 1; every image is named by some block. `image_counts`: the leading positions of each image's 512 that hold real tokens; some image fills all 512.
All inputs are finite; a program needn't handle non-finite values.
Results may differ from the reference program's by a relative error of at most 0.015.
Values may be sent and summed in bfloat16 or wider, within the bound.
A program may use at most 64 MiB of HBM per device.

```python
import jax
import jax.numpy as jnp
from jax import lax

H = 64
KVH = 8
DH = 128
SLOT = 512
IMAGES = 4
BLK = 128
TEXT = 4096
NBLK = 32


def draw_queries(key, part):
    key = jax.random.fold_in(key, 1)
    key_one = jax.random.fold_in(key, 0)
    values_all = jnp.clip(1.5 * jax.random.normal(key_one, (TEXT, H, DH), jnp.float32), -8.0, 8.0)
    return values_all.reshape(TEXT, H * DH).astype(jnp.bfloat16)


def draw_image_keys(key, part):
    key = jax.random.fold_in(key, 2)
    key_one = jax.random.fold_in(key, 0)
    image_rows = jnp.clip(1.5 * jax.random.normal(key_one, (IMAGES * SLOT, KVH, DH), jnp.float32), -8.0, 8.0)
    return image_rows.reshape(IMAGES * SLOT, KVH * DH).astype(jnp.bfloat16)


def draw_image_counts(key, part):
    key = jax.random.fold_in(key, 3)
    key_one, key_two = jax.random.split(key, 2)
    visible = jax.random.randint(key_one, (IMAGES,), SLOT // 4, SLOT + 1)
    full_image = jax.random.randint(key_two, (), 0, IMAGES)
    return jnp.where(jnp.arange(IMAGES) == full_image, SLOT, visible).astype(jnp.int32)


def shard_levels(rng, dims, shards, smallest, top_value):
    factor_of = 1.0
    for dim, shards_of in shards:
        heights = jax.random.uniform(jax.random.fold_in(jax.random.fold_in(rng, 6), dim), (shards_of,), jnp.float32, smallest / len(shards), top_value / len(shards))
        factor_of = factor_of * jnp.repeat(jnp.exp(heights), dims[dim] // shards_of).reshape((-1,) + (1,) * (len(dims) - 1 - dim))
    return factor_of


def choose_distinct(key, rows, amount, top, lift):
    ranking = jax.random.permutation(jax.random.fold_in(key, 1), amount)
    pull = ranking
    for power in range(3):
        pull = pull * pull // amount
    pull = pull * lift // amount
    lots = jax.random.randint(jax.random.fold_in(key, 2), (rows, amount), 0, 4096) + pull
    holders = jax.random.permutation(jax.random.fold_in(key, 3), rows)[jnp.arange(amount) % rows]
    lots = jnp.where(jnp.arange(rows)[:, None] == holders[None, :], 1 << 14, lots)
    score = lots * amount + jnp.arange(amount)
    return lax.top_k(score.astype(jnp.int32), top)[1].astype(jnp.int32)


def scatter_about(rng, shape, spread, most, cuts=(), kind=jnp.bfloat16):
    array = spread * jax.random.normal(rng, shape, jnp.float32)
    if cuts:
        array = array * shard_levels(rng, shape, cuts, -0.22, 0.18)
    return jnp.clip(array, -most, most).astype(kind)


def setup_inputs(seed: int = 0) -> dict:
    key_of = jax.random.split(jax.random.key(seed), 8)
    queries = draw_queries(jax.random.fold_in(key_of[7], 71), 0)
    image_keys = draw_image_keys(jax.random.fold_in(key_of[7], 71), 0)
    image_values = scatter_about(key_of[2], (IMAGES * SLOT, KVH * DH), 2.0, 12.0, ((0, 4),))
    gate_logit = jnp.clip(jax.random.uniform(key_of[3], (1,), jnp.float32, 0.5, 1.5), 0.5, 1.5)
    block_image = choose_distinct(key_of[4], NBLK, IMAGES, 1, 2048)
    image_counts = draw_image_counts(jax.random.fold_in(key_of[7], 71), 0)
    output_grad = scatter_about(key_of[6], (TEXT, H * DH), 1.0, 6.0, ((0, 32),))
    return {"queries": queries, "image_keys": image_keys, "image_values": image_values, "gate_logit": gate_logit, "block_image": block_image, "image_counts": image_counts, "output_grad": output_grad}


def reference(queries, image_keys, image_values, gate_logit, block_image, image_counts, output_grad):
    groups = H // KVH
    scaling = DH ** -0.5
    factor = jnp.tanh(gate_logit[0])
    out_scaled = (factor * output_grad.astype(jnp.float32)).astype(jnp.bfloat16)
    query_blocks = queries.reshape(NBLK, BLK, KVH, groups, DH)
    grad_blocks = out_scaled.reshape(NBLK, BLK, KVH, groups, DH)
    positions = jnp.arange(SLOT)

    def block_step(totals, block_inputs):
        key_total, value_total = totals
        query_block, grad_block, image_id = block_inputs
        first_row = (image_id * SLOT).astype(jnp.int32)
        key_rows = lax.dynamic_slice_in_dim(image_keys, first_row, SLOT, 0)
        value_rows = lax.dynamic_slice_in_dim(image_values, first_row, SLOT, 0)
        key_wide = key_rows.reshape(SLOT, KVH, DH).astype(jnp.float32)
        value_wide = value_rows.reshape(SLOT, KVH, DH).astype(jnp.float32)
        query_wide = query_block.astype(jnp.float32)
        grad_wide = grad_block.astype(jnp.float32)
        visible = positions < image_counts[image_id]
        scores = jnp.einsum("tjgd,ijd->jgti", query_wide, key_wide) * scaling
        scores = jnp.where(visible, scores, -jnp.inf)
        exponent = jnp.exp(scores - jnp.max(scores, axis=-1, keepdims=True))
        weights = exponent / jnp.sum(exponent, axis=-1, keepdims=True)
        weights_low = weights.astype(jnp.bfloat16)
        low_wide = weights_low.astype(jnp.float32)
        mixture = jnp.einsum("jgti,ijd->tjgd", low_wide, value_wide)
        attended = (factor * mixture).astype(jnp.bfloat16)
        value_term = jnp.einsum("jgti,tjgd->ijd", low_wide, grad_wide)
        weight_grad = jnp.einsum("tjgd,ijd->jgti", grad_wide, value_wide)
        centre = jnp.sum(weights * weight_grad, axis=-1, keepdims=True)
        score_grad = (weights * (weight_grad - centre) * scaling).astype(jnp.bfloat16)
        score_wide = score_grad.astype(jnp.float32)
        query_term = jnp.einsum("jgti,ijd->tjgd", score_wide, key_wide).astype(jnp.bfloat16)
        key_term = jnp.einsum("jgti,tjgd->ijd", score_wide, query_wide)
        key_old = lax.dynamic_slice_in_dim(key_total, first_row, SLOT, 0)
        key_total = lax.dynamic_update_slice_in_dim(key_total, key_old + key_term.reshape(SLOT, KVH * DH), first_row, 0)
        value_old = lax.dynamic_slice_in_dim(value_total, first_row, SLOT, 0)
        value_total = lax.dynamic_update_slice_in_dim(value_total, value_old + value_term.reshape(SLOT, KVH * DH), first_row, 0)
        return (key_total, value_total), (attended.reshape(BLK, H * DH), query_term.reshape(BLK, H * DH))

    zeros_total = jnp.zeros((IMAGES * SLOT, KVH * DH), jnp.float32)
    images = block_image[:, 0].astype(jnp.int32)
    totals, outputs = lax.scan(block_step, (zeros_total, zeros_total), (query_blocks, grad_blocks, images))
    attended = outputs[0].reshape(TEXT, H * DH)
    query_grad = outputs[1].reshape(TEXT, H * DH)
    return attended, query_grad, totals[0].astype(jnp.bfloat16), totals[1].astype(jnp.bfloat16)
```

```python
import functools
import math

import jax
import jax.numpy as jnp
from jax import lax
from jax.experimental import pallas as pl
from jax.experimental.pallas import tpu as pltpu
from jax.sharding import PartitionSpec as P

KVH = 8
DH = 128
SLOT = 512
IMAGES = 4
BLK = 128
GROUPS = 8
PAIR = 2
SCALE = DH**-0.5
LOG2E = math.log2(math.e)

ROWS = (((1,), (1,)), ((), ()))


def dot(a, b, dims=(((1,), (0,)), ((), ()))):
    return lax.dot_general(a, b, dims, preferred_element_type=jnp.float32)


def attend(ids, counts, gate_ref, q_ref, g_ref, k_ref, v_ref, o_ref, dq_ref, dkv_ref):
    count = counts[ids[pl.program_id(0)]]
    factor = jnp.tanh(jnp.full((1, DH), gate_ref[0], jnp.float32))
    keys, values = k_ref[...], v_ref[...]
    keys_t, values_t = keys.T, values.T
    wide = PAIR * BLK
    visible = lax.broadcasted_iota(jnp.int32, (SLOT, wide), 0) < count
    dk = jnp.zeros((SLOT, DH), jnp.float32)
    dv = jnp.zeros((SLOT, DH), jnp.float32)
    for first in range(0, GROUPS, PAIR):
        heads = [slice(h * DH, (h + 1) * DH) for h in range(first, first + PAIR)]
        q = jnp.concatenate([q_ref[:, h] for h in heads], axis=0)
        g = jnp.concatenate(
            [(g_ref[:, h].astype(jnp.float32) * factor).astype(jnp.bfloat16) for h in heads], axis=0
        )
        scores = jnp.where(visible, dot(keys, q, ROWS), -jnp.inf)
        top = jnp.max(scores, axis=0, keepdims=True)
        expo = jnp.exp2((scores - top) * (SCALE * LOG2E))
        weights = expo * (1.0 / jnp.sum(expo, axis=0, keepdims=True))
        low = weights.astype(jnp.bfloat16)
        dv += dot(low, g)
        o_t = dot(values_t, low)
        wgrad = dot(values, g, ROWS)
        centre = jnp.sum(weights * wgrad, axis=0, keepdims=True)
        sgrad = (weights * (wgrad - centre)).astype(jnp.bfloat16)
        dq_t = dot(keys_t, sgrad)
        dk += dot(sgrad, q)
        for i, h in enumerate(heads):
            cols = slice(i * BLK, (i + 1) * BLK)
            o_ref[:, h] = (o_t[:, cols].T * factor).astype(jnp.bfloat16)
            dq_ref[:, h] = (dq_t[:, cols].T * SCALE).astype(jnp.bfloat16)
    dkv_ref[0, :, :DH] = (dk * SCALE).astype(jnp.bfloat16)
    dkv_ref[0, :, DH:] = dv.astype(jnp.bfloat16)


def attention(ids, counts, gate, q, g, k, v):
    rows = q.shape[0]
    blocks = rows // BLK
    row_spec = pl.BlockSpec((BLK, GROUPS * DH), lambda b, j, ids, counts: (b, j))
    image_spec = pl.BlockSpec((SLOT, DH), lambda b, j, ids, counts: (ids[b], j))
    return pl.pallas_call(
        attend,
        grid_spec=pltpu.PrefetchScalarGridSpec(
            num_scalar_prefetch=2,
            grid=(blocks, KVH),
            in_specs=[
                pl.BlockSpec(memory_space=pltpu.SMEM),
                row_spec,
                row_spec,
                image_spec,
                image_spec,
            ],
            out_specs=[
                row_spec,
                row_spec,
                pl.BlockSpec((1, SLOT, 2 * DH), lambda b, j, ids, counts: (b, 0, j)),
            ],
        ),
        out_shape=[
            jax.ShapeDtypeStruct(q.shape, jnp.bfloat16),
            jax.ShapeDtypeStruct(q.shape, jnp.bfloat16),
            jax.ShapeDtypeStruct((blocks, SLOT, 2 * KVH * DH), jnp.bfloat16),
        ],
        compiler_params=pltpu.CompilerParams(vmem_limit_bytes=40 << 20),
        cost_estimate=pl.CostEstimate(
            flops=12 * rows * KVH * GROUPS * SLOT * DH,
            bytes_accessed=16 << 20,
            transcendentals=rows * KVH * GROUPS * SLOT,
        ),
    )(ids, counts, gate, q, g, k, v)


def per_device(queries, image_keys, image_values, gate_logit, block_image, image_counts, output_grad):
    grp, seq = lax.axis_size("grp"), lax.axis_size("seq")
    keys = lax.all_gather(image_keys, "grp", axis=0, tiled=True)
    values = lax.all_gather(image_values, "grp", axis=0, tiled=True)
    blocks = queries.shape[0] // BLK
    ids_all = lax.all_gather(block_image[:, 0], "grp", axis=0, tiled=True).reshape(grp, seq, blocks)
    ids_here = lax.dynamic_index_in_dim(ids_all, lax.axis_index("seq"), 1, keepdims=False)
    ids = lax.dynamic_slice_in_dim(block_image[:, 0], lax.axis_index("seq") * blocks, blocks, 0)
    attended, query_grad, dkv = attention(
        ids, image_counts, gate_logit, queries, output_grad, keys, values
    )
    cols = dkv.shape[2] // grp
    parts = lax.all_to_all(
        dkv.reshape(blocks, SLOT, grp, cols), "grp", split_axis=2, concat_axis=0, tiled=True
    )
    parts = parts.reshape(grp * blocks, SLOT, cols)
    flat_ids = ids_here.reshape(grp * blocks)
    picked = [
        jnp.where((flat_ids == m)[:, None, None], parts.astype(jnp.float32), 0.0).sum(0)
        for m in range(IMAGES)
    ]
    out_rows = IMAGES * SLOT // (grp * seq)
    dense = jnp.stack(picked).astype(jnp.bfloat16).reshape(grp, seq, out_rows, cols)
    mine = lax.psum_scatter(dense, "seq", scatter_dimension=1, tiled=True)
    mine = mine.reshape(grp, out_rows, cols)
    whole = lax.all_to_all(mine, "grp", split_axis=0, concat_axis=0, tiled=True)
    whole = whole.transpose(1, 0, 2).reshape(out_rows, KVH, 2, DH)
    key_grad = whole[:, :, 0].reshape(out_rows, KVH * DH)
    value_grad = whole[:, :, 1].reshape(out_rows, KVH * DH)
    return attended, query_grad, key_grad, value_grad


def solution(mesh):
    rows = P(("grp", "seq"), None)
    return jax.shard_map(
        per_device,
        mesh=mesh,
        in_specs=(rows, P("grp", None), P("grp", None), P(), P("grp", None), P(), rows),
        out_specs=(rows, rows, rows, rows),
        check_vma=False,
    )
```

```python
import functools
import math

import jax
import jax.numpy as jnp
from jax import lax
from jax.experimental import pallas as pl
from jax.experimental.pallas import tpu as pltpu
from jax.sharding import PartitionSpec as P

KVH = 8
DH = 128
SLOT = 512
IMAGES = 4
BLK = 128
GROUPS = 8
PAIR = 2
SCALE = DH**-0.5
LOG2E = math.log2(math.e)
MESH = pl.DeviceIdType.MESH

ROWS = (((1,), (1,)), ((), ()))


def dot(a, b, dims=(((1,), (0,)), ((), ()))):
    return lax.dot_general(a, b, dims, preferred_element_type=jnp.float32)


def remote(src, dst, send, recv, device):
    return pltpu.make_async_remote_copy(
        src_ref=src, dst_ref=dst, send_sem=send, recv_sem=recv, device_id=device, device_id_type=MESH
    )


def kernel(
    G, S,
    ids_ref, counts_ref, gate_ref, q_ref, g_ref, k_ref, v_ref,
    o_ref, dq_ref, grads_ref,
    kv, idbuf, parts, landed, zsend, zrecv, fsend,
    id_send, id_recv, sib_send, sib_recv, y_send, y_recv, ys_send, ys_recv,
    x_send, x_recv, xs_send, xs_recv, p_send, p_recv, z_send, z_recv, f_send, f_recv,
):
    C, Z = G // 2, S // 2
    GPI = G // IMAGES
    g, s = lax.axis_index("grp"), lax.axis_index("seq")
    c, k = g // 2, g % 2
    zz, x = s // 2, s % 2
    sib = (c * 2 + (1 - k), s)
    xnb = (g, zz * 2 + (1 - x))
    peers = [((g + d // 2) % G, zz * 2 + (x + d) % 2) for d in range(1, 2 * G)]
    zpeers = [(g, ((zz + d) % Z) * 2 + x) for d in range(1, Z)]

    half = k_ref.shape[0] // 2
    for j in range(KVH):
        for h in range(2):
            kv[j, g, h, 0] = k_ref[h * half : (h + 1) * half, j * DH : (j + 1) * DH]
            kv[j, g, h, 1] = v_ref[h * half : (h + 1) * half, j * DH : (j + 1) * DH]
    own = ids_ref[s, 0]
    me = g * 2 + x
    idbuf[me] = jnp.full((8, DH), own, jnp.int32)

    barrier = pltpu.get_barrier_semaphore()
    for device in peers + zpeers:
        pl.semaphore_signal(barrier, inc=1, device_id=device, device_id_type=MESH)
    pl.semaphore_wait(barrier, len(peers) + len(zpeers))

    def sib_copy(j):
        return remote(kv.at[j, g], kv.at[j, g], sib_send.at[j], sib_recv.at[j], sib)

    def y_copy(j, d):
        to = (((c + d) % C) * 2 + k, s)
        return remote(kv.at[j, g, x], kv.at[j, g, x], y_send.at[j, d - 1], y_recv.at[j, d - 1], to)

    def source(d):
        return ((c + C - d) % C) * 2 + k

    def ys_copy(j, d):
        ref = kv.at[j, source(d), x]
        return remote(ref, ref, ys_send.at[j, d - 1], ys_recv.at[j, d - 1], sib)

    def x_copy(j, d):
        ref = kv.at[j, source(d), x]
        return remote(ref, ref, x_send.at[j, d - 1], x_recv.at[j, d - 1], xnb)

    def xs_copy(j, d):
        ref = kv.at[j, source(d), 1 - x]
        return remote(ref, ref, xs_send.at[j, d - 1], xs_recv.at[j, d - 1], sib)

    def id_copy(i):
        return remote(idbuf.at[me], idbuf.at[me], id_send.at[i], id_recv.at[i], peers[i])

    @pl.loop(0, KVH)
    def _(j):
        for d in range(1, C):
            y_copy(j, d).start()
        sib_copy(j).start()

    for i in range(len(peers)):
        id_copy(i).start()

    def y_forward(j):
        for d in range(1, C):
            y_copy(j, d).wait_recv()
            x_copy(j, d).start()
            ys_copy(j, d).start()

    def x_forward(j):
        for d in range(1, C):
            x_copy(j, d).wait_recv()
            xs_copy(j, d).start()

    y_forward(0)
    y_forward(1)
    x_forward(0)
    for i in range(len(peers)):
        id_copy(i).wait()

    count = counts_ref[0]
    for m in range(1, IMAGES):
        count = jnp.where(own == m, counts_ref[m], count)
    factor = jnp.tanh(jnp.full((1, DH), gate_ref[0], jnp.float32))

    def image_of(j, t):
        rows = []
        for i in range(GPI):
            for h in range(2):
                part = kv[j, i, h, t]
                for m in range(1, IMAGES):
                    part = jnp.where(own == m, kv[j, m * GPI + i, h, t], part)
                rows.append(part)
        return jnp.concatenate(rows, axis=0)

    def piece_copy(j, t, to_x):
        to = ((j % C) * 2 + t, zz * 2 + to_x)
        a = j // C
        return remote(
            parts.at[j, t, to_x], landed.at[a, me], p_send.at[j, t, to_x], p_recv.at[a, me], to
        )

    def piece_local(j):
        a = j // C
        return pltpu.make_async_copy(parts.at[j, k, x], landed.at[a, me], p_recv.at[a, me])

    def compute(j):
        keys, values = image_of(j, 0), image_of(j, 1)
        keys_t, values_t = keys.T, values.T
        wide = PAIR * BLK
        visible = lax.broadcasted_iota(jnp.int32, (SLOT, wide), 0) < count
        dk = jnp.zeros((SLOT, DH), jnp.float32)
        dv = jnp.zeros((SLOT, DH), jnp.float32)
        for first in range(0, GROUPS, PAIR):
            heads = [
                pl.ds(pl.multiple_of((j * GROUPS + h) * DH, DH), DH)
                for h in range(first, first + PAIR)
            ]
            q = jnp.concatenate([q_ref[:, h] for h in heads], axis=0)
            gr = jnp.concatenate(
                [(g_ref[:, h].astype(jnp.float32) * factor).astype(jnp.bfloat16) for h in heads],
                axis=0,
            )
            scores = jnp.where(visible, dot(keys, q, ROWS), -jnp.inf)
            top = jnp.max(scores, axis=0, keepdims=True)
            expo = jnp.exp2((scores - top) * (SCALE * LOG2E))
            weights = expo * (1.0 / jnp.sum(expo, axis=0, keepdims=True))
            low = weights.astype(jnp.bfloat16)
            dv += dot(low, gr)
            o_t = dot(values_t, low)
            wgrad = dot(values, gr, ROWS)
            centre = jnp.sum(weights * wgrad, axis=0, keepdims=True)
            sgrad = (weights * (wgrad - centre)).astype(jnp.bfloat16)
            dq_t = dot(keys_t, sgrad)
            dk += dot(sgrad, q)
            for i, h in enumerate(heads):
                cols = slice(i * BLK, (i + 1) * BLK)
                o_ref[:, h] = (o_t[:, cols].T * factor).astype(jnp.bfloat16)
                dq_ref[:, h] = (dq_t[:, cols].T * SCALE).astype(jnp.bfloat16)
        rr = SLOT // (GPI * S)
        for t, total in ((0, dk * SCALE), (1, dv)):
            total = total.reshape(GPI, Z, 2, rr, DH).astype(jnp.bfloat16)
            for to_x in range(2):
                parts[j, t, to_x] = total[:, :, to_x]

    def start_pieces(j):
        mine = j % C == c
        for t in range(2):
            for to_x in range(2):
                here = mine & (k == t) & (x == to_x)

                @pl.when(jnp.logical_not(here))
                def _():
                    piece_copy(j, t, to_x).start()

        @pl.when(mine)
        def _():
            piece_local(j).start()

    def wait_sent_pieces(j):
        mine = j % C == c
        for t in range(2):
            for to_x in range(2):
                here = mine & (k == t) & (x == to_x)

                @pl.when(jnp.logical_not(here))
                def _():
                    piece_copy(j, t, to_x).wait_send()

    def z_copy(a, d):
        to = (zz + d) % Z
        return remote(
            zsend.at[a, to], zrecv.at[a, d - 1], z_send.at[a, d - 1], z_recv.at[a, d - 1],
            (g, to * 2 + x),
        )

    def sum_images(j):
        a = j // C

        @pl.loop(0, 2 * G)
        def _(p):
            pltpu.make_async_copy(parts.at[0, 0, 0], landed.at[a, p], p_recv.at[a, p]).wait()

        @pl.loop(0, Z)
        def _(zt):
            sums = [None] * IMAGES
            for p in range(2 * G):
                piece = landed[a, p, :, zt].astype(jnp.float32)
                who = idbuf[p][0:1].reshape(1, 1, DH)
                for m in range(IMAGES):
                    term = jnp.where(who == m, piece, 0.0)
                    sums[m] = term if p == 0 else sums[m] + term
            for m in range(IMAGES):
                zsend[a, zt, m] = sums[m].astype(jnp.bfloat16)

        for d in range(1, Z):
            z_copy(a, d).start()

    def f_copy(a, d):
        to = (g + d) % G
        return remote(
            fsend.at[a, to], grads_ref.at[a, g], f_send.at[a, d - 1], f_recv.at[a, d - 1], (to, s)
        )

    def sum_z(j):
        a = j // C
        for d in range(1, Z):
            z_copy(a, d).wait_recv()
        total = zsend[a, zz].astype(jnp.float32)
        for d in range(1, Z):
            total += zrecv[a, d - 1].astype(jnp.float32)
        total = total.astype(jnp.bfloat16)
        for m in range(IMAGES):
            for i in range(GPI):
                fsend[a, m * GPI + i] = total[m, i]
        grads_ref[a, g] = fsend[a, g]
        for d in range(1, G):
            f_copy(a, d).start()

    @pl.loop(0, KVH + 2)
    def _(j):
        @pl.when(j < KVH)
        def _():
            @pl.when(j + 2 < KVH)
            def _():
                y_forward(j + 2)

            @pl.when(j + 1 < KVH)
            def _():
                x_forward(j + 1)

            sib_copy(j).wait_recv()
            for d in range(1, C):
                ys_copy(j, d).wait_recv()
                xs_copy(j, d).wait_recv()
            compute(j)
            start_pieces(j)

        @pl.when((j >= 1) & (j <= KVH) & ((j + C - 1) % C == c))
        def _():
            sum_images(j - 1)

        @pl.when((j >= 2) & ((j + 2 * C - 2) % C == c))
        def _():
            sum_z(j - 2)

    @pl.loop(0, KVH // C)
    def _(a):
        for d in range(1, G):
            f_copy(a, d).wait()
        for d in range(1, Z):
            z_copy(a, d).wait_send()

    @pl.loop(0, KVH)
    def _(j):
        sib_copy(j).wait_send()
        for d in range(1, C):
            y_copy(j, d).wait_send()
            ys_copy(j, d).wait_send()
            x_copy(j, d).wait_send()
            xs_copy(j, d).wait_send()
        wait_sent_pieces(j)


def per_device(queries, image_keys, image_values, gate_logit, block_image, image_counts, output_grad):
    G, S = lax.axis_size("grp"), lax.axis_size("seq")
    C, Z, GPI = G // 2, S // 2, G // IMAGES
    rows = queries.shape[0]
    assert rows == BLK and 2 * KVH % G == 0
    A = KVH // C
    rr = SLOT // (GPI * S)
    half = image_keys.shape[0] // 2
    smem = pl.BlockSpec(memory_space=pltpu.SMEM)
    vmem = pl.BlockSpec(memory_space=pltpu.VMEM)
    dma = pltpu.SemaphoreType.DMA
    bf16 = jnp.bfloat16
    attended, query_grad, grads = pl.pallas_call(
        functools.partial(kernel, G, S),
        in_specs=[smem] * 3 + [vmem] * 4,
        out_specs=[vmem] * 3,
        out_shape=[
            jax.ShapeDtypeStruct(queries.shape, bf16),
            jax.ShapeDtypeStruct(queries.shape, bf16),
            jax.ShapeDtypeStruct((A, G, rr, DH), bf16),
        ],
        scratch_shapes=[
            pltpu.VMEM((KVH, G, 2, 2, half, DH), bf16),
            pltpu.VMEM((2 * G, 8, DH), jnp.int32),
            pltpu.VMEM((KVH, 2, 2, GPI, Z, rr, DH), bf16),
            pltpu.VMEM((A, 2 * G, GPI, Z, rr, DH), bf16),
            pltpu.VMEM((A, Z, IMAGES, GPI, rr, DH), bf16),
            pltpu.VMEM((A, Z - 1, IMAGES, GPI, rr, DH), bf16),
            pltpu.VMEM((A, G, rr, DH), bf16),
            dma((2 * G - 1,)), dma((2 * G - 1,)),
            dma((KVH,)), dma((KVH,)),
        ]
        + [dma((KVH, C - 1))] * 8
        + [
            dma((KVH, 2, 2)), dma((A, 2 * G)),
            dma((A, Z - 1)), dma((A, Z - 1)),
            dma((A, G - 1)), dma((A, G - 1)),
        ],
        compiler_params=pltpu.CompilerParams(
            collective_id=0, has_side_effects=True, vmem_limit_bytes=48 << 20
        ),
        cost_estimate=pl.CostEstimate(
            flops=12 * rows * KVH * GROUPS * SLOT * DH,
            bytes_accessed=16 << 20,
            transcendentals=rows * KVH * GROUPS * SLOT,
        ),
    )(block_image, image_counts, gate_logit, queries, output_grad, image_keys, image_values)
    grads = grads.reshape(KVH, 2, rr, DH).transpose(1, 2, 0, 3).reshape(2, rr, KVH * DH)
    return attended, query_grad, grads[0], grads[1]


def solution(mesh):
    rows = P(("grp", "seq"), None)
    return jax.shard_map(
        per_device,
        mesh=mesh,
        in_specs=(rows, P("grp", None), P("grp", None), P(), P("grp", None), P(), rows),
        out_specs=(rows, rows, rows, rows),
        check_vma=False,
    )
```

```python
import functools
import math

import jax
import jax.numpy as jnp
from jax import lax
from jax.experimental import pallas as pl
from jax.experimental.pallas import tpu as pltpu
from jax.sharding import PartitionSpec as P

KVH = 8
DH = 128
SLOT = 512
IMAGES = 4
BLK = 128
GROUPS = 8
PAIR = 2
SCALE = DH**-0.5
LOG2E = math.log2(math.e)
MESH = pl.DeviceIdType.MESH

ROWS = (((1,), (1,)), ((), ()))


def dot(a, b, dims=(((1,), (0,)), ((), ()))):
    return lax.dot_general(a, b, dims, preferred_element_type=jnp.float32)


def remote(src, dst, send, recv, device):
    return pltpu.make_async_remote_copy(
        src_ref=src, dst_ref=dst, send_sem=send, recv_sem=recv, device_id=device, device_id_type=MESH
    )


def kernel(
    G, S,
    ids_ref, counts_ref, gate_ref, q_hbm, g_hbm, k_ref, v_ref,
    o_ref, dq_ref, grads_ref,
    q_ref, g_ref, in_sem, kv, idbuf, parts, landed, zsend, zrecv, fsend,
    id_send, id_recv, sib_send, sib_recv, y_send, y_recv, ys_send, ys_recv,
    x_send, x_recv, xs_send, xs_recv, p_send, p_recv, z_send, z_recv, f_send, f_recv,
):
    C, Z = G // 2, S // 2
    GPI = G // IMAGES
    g, s = lax.axis_index("grp"), lax.axis_index("seq")
    c, k = g // 2, g % 2
    zz, x = s // 2, s % 2
    sib = (c * 2 + (1 - k), s)
    xnb = (g, zz * 2 + (1 - x))
    peers = [((g + d // 2) % G, zz * 2 + (x + d) % 2) for d in range(1, 2 * G)]
    zpeers = [(g, ((zz + d) % Z) * 2 + x) for d in range(1, Z)]

    loads = [
        pltpu.make_async_copy(src, dst, in_sem.at[i])
        for i, (src, dst) in enumerate(((q_hbm, q_ref), (g_hbm, g_ref)))
    ]
    for load in loads:
        load.start()
    half = k_ref.shape[0] // 2
    own = ids_ref[s, 0]
    me = g * 2 + x
    idbuf[me] = jnp.full((8, DH), own, jnp.int32)

    barrier = pltpu.get_barrier_semaphore()
    for device in peers + zpeers:
        pl.semaphore_signal(barrier, inc=1, device_id=device, device_id_type=MESH)
    pl.semaphore_wait(barrier, len(peers) + len(zpeers))

    def sib_copy(j):
        return remote(kv.at[j, g], kv.at[j, g], sib_send.at[j], sib_recv.at[j], sib)

    def y_copy(j, d):
        to = (((c + d) % C) * 2 + k, s)
        return remote(kv.at[j, g, x], kv.at[j, g, x], y_send.at[j, d - 1], y_recv.at[j, d - 1], to)

    def source(d):
        return ((c + C - d) % C) * 2 + k

    def ys_copy(j, d):
        ref = kv.at[j, source(d), x]
        return remote(ref, ref, ys_send.at[j, d - 1], ys_recv.at[j, d - 1], sib)

    def x_copy(j, d):
        ref = kv.at[j, source(d), x]
        return remote(ref, ref, x_send.at[j, d - 1], x_recv.at[j, d - 1], xnb)

    def xs_copy(j, d):
        ref = kv.at[j, source(d), 1 - x]
        return remote(ref, ref, xs_send.at[j, d - 1], xs_recv.at[j, d - 1], sib)

    def id_copy(i):
        return remote(idbuf.at[me], idbuf.at[me], id_send.at[i], id_recv.at[i], peers[i])

    def issue(j):
        cols = pl.ds(pl.multiple_of(j * DH, DH), DH)
        for h in range(2):
            kv[j, g, h, 0] = k_ref[h * half : (h + 1) * half, cols]
            kv[j, g, h, 1] = v_ref[h * half : (h + 1) * half, cols]
        for d in range(1, C):
            y_copy(j, d).start()
        sib_copy(j).start()

    def y_forward(j):
        for d in range(1, C):
            y_copy(j, d).wait_recv()
            x_copy(j, d).start()
            ys_copy(j, d).start()

    def x_forward(j):
        for d in range(1, C):
            x_copy(j, d).wait_recv()
            xs_copy(j, d).start()

    issue(0)
    issue(1)
    y_forward(0)
    issue(2)
    y_forward(1)
    issue(3)
    for i in range(len(peers)):
        id_copy(i).start()
    x_forward(0)
    for load in loads:
        load.wait()

    count = counts_ref[0]
    for m in range(1, IMAGES):
        count = jnp.where(own == m, counts_ref[m], count)
    factor = jnp.tanh(jnp.full((1, DH), gate_ref[0], jnp.float32))

    def image_of(j, t):
        rows = []
        for i in range(GPI):
            for h in range(2):
                part = kv[j, i, h, t]
                for m in range(1, IMAGES):
                    part = jnp.where(own == m, kv[j, m * GPI + i, h, t], part)
                rows.append(part)
        return jnp.concatenate(rows, axis=0)

    def piece_copy(j, t, to_x):
        to = ((j % C) * 2 + t, zz * 2 + to_x)
        a = j // C
        return remote(
            parts.at[j, t, to_x], landed.at[a, me], p_send.at[j, t, to_x], p_recv.at[a, me], to
        )

    def piece_local(j):
        a = j // C
        return pltpu.make_async_copy(parts.at[j, k, x], landed.at[a, me], p_recv.at[a, me])

    def compute(j):
        keys, values = image_of(j, 0), image_of(j, 1)
        keys_t, values_t = keys.T, values.T
        wide = PAIR * BLK
        visible = lax.broadcasted_iota(jnp.int32, (SLOT, wide), 0) < count
        dk = jnp.zeros((SLOT, DH), jnp.float32)
        dv = jnp.zeros((SLOT, DH), jnp.float32)
        for first in range(0, GROUPS, PAIR):
            heads = [
                pl.ds(pl.multiple_of((j * GROUPS + h) * DH, DH), DH)
                for h in range(first, first + PAIR)
            ]
            q = jnp.concatenate([q_ref[:, h] for h in heads], axis=0)
            gr = jnp.concatenate(
                [(g_ref[:, h].astype(jnp.float32) * factor).astype(jnp.bfloat16) for h in heads],
                axis=0,
            )
            scores = jnp.where(visible, dot(keys, q, ROWS), -jnp.inf)
            top = jnp.max(scores, axis=0, keepdims=True)
            expo = jnp.exp2((scores - top) * (SCALE * LOG2E))
            weights = expo * (1.0 / jnp.sum(expo, axis=0, keepdims=True))
            low = weights.astype(jnp.bfloat16)
            dv += dot(low, gr)
            o_t = dot(values_t, low)
            wgrad = dot(values, gr, ROWS)
            centre = jnp.sum(weights * wgrad, axis=0, keepdims=True)
            sgrad = (weights * (wgrad - centre)).astype(jnp.bfloat16)
            dq_t = dot(keys_t, sgrad)
            dk += dot(sgrad, q)
            for i, h in enumerate(heads):
                cols = slice(i * BLK, (i + 1) * BLK)
                o_ref[:, h] = (o_t[:, cols].T * factor).astype(jnp.bfloat16)
                dq_ref[:, h] = (dq_t[:, cols].T * SCALE).astype(jnp.bfloat16)
        rr = SLOT // (GPI * S)
        for t, total in ((0, dk * SCALE), (1, dv)):
            total = total.reshape(GPI, Z, 2, rr, DH).astype(jnp.bfloat16)
            for to_x in range(2):
                parts[j, t, to_x] = total[:, :, to_x]

    def start_pieces(j):
        mine = j % C == c
        for t in range(2):
            for to_x in range(2):
                here = mine & (k == t) & (x == to_x)

                @pl.when(jnp.logical_not(here))
                def _():
                    piece_copy(j, t, to_x).start()

        @pl.when(mine)
        def _():
            piece_local(j).start()

    def wait_sent_pieces(j):
        mine = j % C == c
        for t in range(2):
            for to_x in range(2):
                here = mine & (k == t) & (x == to_x)

                @pl.when(jnp.logical_not(here))
                def _():
                    piece_copy(j, t, to_x).wait_send()

    def z_copy(a, d):
        to = (zz + d) % Z
        return remote(
            zsend.at[a, to], zrecv.at[a, d - 1], z_send.at[a, d - 1], z_recv.at[a, d - 1],
            (g, to * 2 + x),
        )

    def sum_images(j):
        a = j // C

        @pl.loop(0, 2 * G)
        def _(p):
            pltpu.make_async_copy(parts.at[0, 0, 0], landed.at[a, p], p_recv.at[a, p]).wait()

        @pl.loop(0, Z)
        def _(zt):
            sums = [None] * IMAGES
            for p in range(2 * G):
                piece = landed[a, p, :, zt].astype(jnp.float32)
                who = idbuf[p][0:1].reshape(1, 1, DH)
                for m in range(IMAGES):
                    term = jnp.where(who == m, piece, 0.0)
                    sums[m] = term if p == 0 else sums[m] + term
            for m in range(IMAGES):
                zsend[a, zt, m] = sums[m].astype(jnp.bfloat16)

        for d in range(1, Z):
            z_copy(a, d).start()

    def f_copy(a, d):
        to = (g + d) % G
        return remote(
            fsend.at[a, to], grads_ref.at[a, g], f_send.at[a, d - 1], f_recv.at[a, d - 1], (to, s)
        )

    def sum_z(j):
        a = j // C
        for d in range(1, Z):
            z_copy(a, d).wait_recv()
        total = zsend[a, zz].astype(jnp.float32)
        for d in range(1, Z):
            total += zrecv[a, d - 1].astype(jnp.float32)
        total = total.astype(jnp.bfloat16)
        for m in range(IMAGES):
            for i in range(GPI):
                fsend[a, m * GPI + i] = total[m, i]
        grads_ref[a, g] = fsend[a, g]
        for d in range(1, G):
            f_copy(a, d).start()

    @pl.loop(0, KVH + 4)
    def _(j):
        @pl.when(j < KVH)
        def _():
            @pl.when(j + 2 < KVH)
            def _():
                y_forward(j + 2)

            @pl.when(j + 1 < KVH)
            def _():
                x_forward(j + 1)

            @pl.when(j + 4 < KVH)
            def _():
                issue(j + 4)

            sib_copy(j).wait_recv()
            for d in range(1, C):
                ys_copy(j, d).wait_recv()
                xs_copy(j, d).wait_recv()
            compute(j)
            start_pieces(j)

        @pl.when(j == 1)
        def _():
            for i in range(len(peers)):
                id_copy(i).wait()

        @pl.when((j >= 2) & (j < KVH + 2) & ((j + 2 * C - 2) % C == c))
        def _():
            sum_images(j - 2)

        @pl.when((j >= 4) & ((j + 4 * C - 4) % C == c))
        def _():
            sum_z(j - 4)

    @pl.loop(0, KVH // C)
    def _(a):
        for d in range(1, G):
            f_copy(a, d).wait()
        for d in range(1, Z):
            z_copy(a, d).wait_send()

    @pl.loop(0, KVH)
    def _(j):
        sib_copy(j).wait_send()
        for d in range(1, C):
            y_copy(j, d).wait_send()
            ys_copy(j, d).wait_send()
            x_copy(j, d).wait_send()
            xs_copy(j, d).wait_send()
        wait_sent_pieces(j)


def per_device(queries, image_keys, image_values, gate_logit, block_image, image_counts, output_grad):
    G, S = lax.axis_size("grp"), lax.axis_size("seq")
    C, Z, GPI = G // 2, S // 2, G // IMAGES
    rows = queries.shape[0]
    assert rows == BLK and 2 * KVH % G == 0
    A = KVH // C
    rr = SLOT // (GPI * S)
    half = image_keys.shape[0] // 2
    smem = pl.BlockSpec(memory_space=pltpu.SMEM)
    vmem = pl.BlockSpec(memory_space=pltpu.VMEM)
    hbm = pl.BlockSpec(memory_space=pltpu.HBM)
    dma = pltpu.SemaphoreType.DMA
    bf16 = jnp.bfloat16
    attended, query_grad, grads = pl.pallas_call(
        functools.partial(kernel, G, S),
        in_specs=[smem] * 3 + [hbm] * 2 + [vmem] * 2,
        out_specs=[vmem] * 3,
        out_shape=[
            jax.ShapeDtypeStruct(queries.shape, bf16),
            jax.ShapeDtypeStruct(queries.shape, bf16),
            jax.ShapeDtypeStruct((A, G, rr, DH), bf16),
        ],
        scratch_shapes=[
            pltpu.VMEM(queries.shape, bf16),
            pltpu.VMEM(queries.shape, bf16),
            dma((2,)),
            pltpu.VMEM((KVH, G, 2, 2, half, DH), bf16),
            pltpu.VMEM((2 * G, 8, DH), jnp.int32),
            pltpu.VMEM((KVH, 2, 2, GPI, Z, rr, DH), bf16),
            pltpu.VMEM((A, 2 * G, GPI, Z, rr, DH), bf16),
            pltpu.VMEM((A, Z, IMAGES, GPI, rr, DH), bf16),
            pltpu.VMEM((A, Z - 1, IMAGES, GPI, rr, DH), bf16),
            pltpu.VMEM((A, G, rr, DH), bf16),
            dma((2 * G - 1,)), dma((2 * G - 1,)),
            dma((KVH,)), dma((KVH,)),
        ]
        + [dma((KVH, C - 1))] * 8
        + [
            dma((KVH, 2, 2)), dma((A, 2 * G)),
            dma((A, Z - 1)), dma((A, Z - 1)),
            dma((A, G - 1)), dma((A, G - 1)),
        ],
        compiler_params=pltpu.CompilerParams(
            collective_id=0, has_side_effects=True, vmem_limit_bytes=48 << 20
        ),
        cost_estimate=pl.CostEstimate(
            flops=12 * rows * KVH * GROUPS * SLOT * DH,
            bytes_accessed=16 << 20,
            transcendentals=rows * KVH * GROUPS * SLOT,
        ),
    )(block_image, image_counts, gate_logit, queries, output_grad, image_keys, image_values)
    grads = grads.reshape(KVH, 2, rr, DH).transpose(1, 2, 0, 3).reshape(2, rr, KVH * DH)
    return attended, query_grad, grads[0], grads[1]


def solution(mesh):
    rows = P(("grp", "seq"), None)
    return jax.shard_map(
        per_device,
        mesh=mesh,
        in_specs=(rows, P("grp", None), P("grp", None), P(), P("grp", None), P(), rows),
        out_specs=(rows, rows, rows, rows),
        check_vma=False,
    )
```

```python
import functools
import math

import jax
import jax.numpy as jnp
from jax import lax
from jax.experimental import pallas as pl
from jax.experimental.pallas import tpu as pltpu
from jax.sharding import PartitionSpec as P

KVH = 8
DH = 128
SLOT = 512
IMAGES = 4
BLK = 128
GROUPS = 8
PAIR = 4
SCALE = DH**-0.5
LOG2E = math.log2(math.e)
MESH = pl.DeviceIdType.MESH

ROWS = (((1,), (1,)), ((), ()))


def dot(a, b, dims=(((1,), (0,)), ((), ()))):
    return lax.dot_general(a, b, dims, preferred_element_type=jnp.float32)


def remote(src, dst, send, recv, device):
    return pltpu.make_async_remote_copy(
        src_ref=src, dst_ref=dst, send_sem=send, recv_sem=recv, device_id=device, device_id_type=MESH
    )


def kernel(
    G, S,
    ids_ref, counts_ref, gate_ref, q_hbm, g_hbm, k_hbm, v_hbm,
    o_ref, dq_ref, grads_ref,
    q_ref, g_ref, k_ref, v_ref, in_sem, kv, idbuf, parts, landed, zsend, zrecv, fsend,
    id_send, id_recv, sib_send, sib_recv, y_send, y_recv, x_send, x_recv, z1_send, z1_recv,
    xz_send, xz_recv, zx_send, zx_recv, fwd_send, fwd_recv, p_send, p_recv, z_send, z_recv, f_send, f_recv,
):
    C, Z = G // 2, S // 2
    GPI = G // IMAGES
    g, s = lax.axis_index("grp"), lax.axis_index("seq")
    c, k = g // 2, g % 2
    zz, x = s // 2, s % 2
    sib = (c * 2 + (1 - k), s)
    zb = zz % 2
    xnb = (g, zz * 2 + (1 - x))
    znb = (g, (zz + 1 - 2 * zb) * 2 + x)
    peers = [((g + d // 2) % G, zz * 2 + (x + d) % 2) for d in range(1, 2 * G)]
    zpeers = [(g, ((zz + d) % Z) * 2 + x) for d in range(1, Z)]

    loads = [
        pltpu.make_async_copy(src, dst, in_sem.at[i])
        for i, (src, dst) in enumerate(
            ((k_hbm, k_ref), (v_hbm, v_ref), (q_hbm, q_ref), (g_hbm, g_ref))
        )
    ]
    for load in loads:
        load.start()
    eighth = k_ref.shape[0] // 8
    own = ids_ref[s, 0]
    me = g * 2 + x
    idbuf[me] = jnp.full((8, DH), own, jnp.int32)

    barrier = pltpu.get_barrier_semaphore()
    for device in peers + zpeers:
        pl.semaphore_signal(barrier, inc=1, device_id=device, device_id_type=MESH)
    pl.semaphore_wait(barrier, len(peers) + len(zpeers))

    def sib_copy(j):
        return remote(kv.at[j, g], kv.at[j, g], sib_send.at[j], sib_recv.at[j], sib)

    def source(d):
        return ((c + C - d) % C) * 2 + k

    def copy(ref, sems, j, d, to):
        return remote(ref, ref, sems[0].at[j, d - 1], sems[1].at[j, d - 1], to)

    def y_copy(j, d):
        to = (((c + d) % C) * 2 + k, s)
        return copy(kv.at[j, g, x, zb], (y_send, y_recv), j, d, to)

    def x_copy(j, d):
        return copy(kv.at[j, source(d), x, zb], (x_send, x_recv), j, d, xnb)

    def z1_copy(j, d):
        return copy(kv.at[j, source(d), x, zb], (z1_send, z1_recv), j, d, znb)

    def xz_copy(j, d):
        return copy(kv.at[j, source(d), 1 - x, zb, 0], (xz_send, xz_recv), j, d, znb)

    def zx_copy(j, d):
        return copy(kv.at[j, source(d), x, 1 - zb, 1], (zx_send, zx_recv), j, d, xnb)

    def fwd_copy(j, d, xh, zh):
        return copy(kv.at[j, source(d), xh, zh], (fwd_send, fwd_recv), j, d, sib)

    def fwd_all(j, d):
        return copy(kv.at[j, source(d)], (fwd_send, fwd_recv), j, d, sib)

    def id_copy(i):
        return remote(idbuf.at[me], idbuf.at[me], id_send.at[i], id_recv.at[i], peers[i])

    def issue(j):
        cols = pl.ds(pl.multiple_of(j * DH, DH), DH)
        for i in range(8):
            part = slice(i * eighth, (i + 1) * eighth)
            kv[j, g, i // 4, i // 2 % 2, i % 2, 0] = k_ref[part, cols]
            kv[j, g, i // 4, i // 2 % 2, i % 2, 1] = v_ref[part, cols]
        for d in range(1, C):
            y_copy(j, d).start()
        sib_copy(j).start()

    def y_forward(j):
        for d in range(1, C):
            y_copy(j, d).wait_recv()
            x_copy(j, d).start()
            z1_copy(j, d).start()
            fwd_copy(j, d, x, zb).start()

    def xz_forward(j):
        for d in range(1, C):
            x_copy(j, d).wait_recv()
            xz_copy(j, d).start()
            fwd_copy(j, d, 1 - x, zb).start()
            z1_copy(j, d).wait_recv()
            zx_copy(j, d).start()
            fwd_copy(j, d, x, 1 - zb).start()

    def last_forward(j):
        for d in range(1, C):
            xz_copy(j, d).wait_recv()
            zx_copy(j, d).wait_recv()
            fwd_copy(j, d, 1 - x, 1 - zb).start()

    for load in loads[:2]:
        load.wait()
    issue(0)
    issue(1)
    y_forward(0)
    issue(2)
    y_forward(1)
    xz_forward(0)
    issue(3)
    y_forward(2)
    issue(4)
    for i in range(len(peers)):
        id_copy(i).start()
    xz_forward(1)
    last_forward(0)
    for load in loads[2:]:
        load.wait()

    count = counts_ref[0]
    for m in range(1, IMAGES):
        count = jnp.where(own == m, counts_ref[m], count)
    factor = jnp.tanh(jnp.full((1, DH), gate_ref[0], jnp.float32))

    def image_of(j, t):
        rows = []
        for i in range(GPI):
            for n in range(8):
                at = (n // 4, n // 2 % 2, n % 2, t)
                part = kv[(j, i) + at]
                for m in range(1, IMAGES):
                    part = jnp.where(own == m, kv[(j, m * GPI + i) + at], part)
                rows.append(part)
        return jnp.concatenate(rows, axis=0)

    half = C // 2
    kind = c // half

    def owner(j, t):
        return (t * half + j // 2 % half) * 2 + j % 2

    def piece_copy(j, t, to_x):
        to = (owner(j, t), zz * 2 + to_x)
        a = j // C
        return remote(
            parts.at[j, t, to_x], landed.at[a, me], p_send.at[j, t, to_x], p_recv.at[a, me], to
        )

    def piece_local(j):
        a = j // C
        return pltpu.make_async_copy(parts.at[j, kind, x], landed.at[a, me], p_recv.at[a, me])

    def compute(j):
        keys, values = image_of(j, 0), image_of(j, 1)
        keys_t, values_t = keys.T, values.T
        wide = PAIR * BLK
        visible = lax.broadcasted_iota(jnp.int32, (SLOT, wide), 0) < count
        dk = jnp.zeros((SLOT, DH), jnp.float32)
        dv = jnp.zeros((SLOT, DH), jnp.float32)
        for first in range(0, GROUPS, PAIR):
            heads = [
                pl.ds(pl.multiple_of((j * GROUPS + h) * DH, DH), DH)
                for h in range(first, first + PAIR)
            ]
            q = jnp.concatenate([q_ref[:, h] for h in heads], axis=0)
            gr = jnp.concatenate(
                [(g_ref[:, h].astype(jnp.float32) * factor).astype(jnp.bfloat16) for h in heads],
                axis=0,
            )
            scores = jnp.where(visible, dot(keys, q, ROWS), -jnp.inf)
            top = jnp.max(scores, axis=0, keepdims=True)
            expo = jnp.exp2((scores - top) * (SCALE * LOG2E))
            weights = expo * (1.0 / jnp.sum(expo, axis=0, keepdims=True))
            low = weights.astype(jnp.bfloat16)
            dv += dot(low, gr)
            o_t = dot(values_t, low)
            wgrad = dot(values, gr, ROWS)
            centre = jnp.sum(weights * wgrad, axis=0, keepdims=True)
            sgrad = (weights * (wgrad - centre)).astype(jnp.bfloat16)
            dq_t = dot(keys_t, sgrad)
            dk += dot(sgrad, q)
            for i, h in enumerate(heads):
                cols = slice(i * BLK, (i + 1) * BLK)
                o_ref[:, h] = (o_t[:, cols].T * factor).astype(jnp.bfloat16)
                dq_ref[:, h] = (dq_t[:, cols].T * SCALE).astype(jnp.bfloat16)
        rr = SLOT // (GPI * S)
        for t, total in ((0, dk * SCALE), (1, dv)):
            total = total.reshape(GPI, Z, 2, rr, DH).astype(jnp.bfloat16)
            for to_x in range(2):
                parts[j, t, to_x] = total[:, :, to_x]

    def start_pieces(j):
        mine = owner(j, kind) == g
        for t in range(2):
            for to_x in range(2):
                here = (owner(j, t) == g) & (x == to_x)

                @pl.when(jnp.logical_not(here))
                def _():
                    piece_copy(j, t, to_x).start()

        @pl.when(mine)
        def _():
            piece_local(j).start()

    def wait_sent_pieces(j):
        mine = owner(j, kind) == g
        for t in range(2):
            for to_x in range(2):
                here = (owner(j, t) == g) & (x == to_x)

                @pl.when(jnp.logical_not(here))
                def _():
                    piece_copy(j, t, to_x).wait_send()

    def z_copy(a, d):
        to = (zz + d) % Z
        return remote(
            zsend.at[a, to], zrecv.at[a, d - 1], z_send.at[a, d - 1], z_recv.at[a, d - 1],
            (g, to * 2 + x),
        )

    def sum_images(j):
        a = j // C

        @pl.loop(0, 2 * G)
        def _(p):
            pltpu.make_async_copy(parts.at[0, 0, 0], landed.at[a, p], p_recv.at[a, p]).wait()

        @pl.loop(0, Z)
        def _(zt):
            sums = [None] * IMAGES
            for p in range(2 * G):
                piece = landed[a, p, :, zt].astype(jnp.float32)
                who = idbuf[p][0:1].reshape(1, 1, DH)
                for m in range(IMAGES):
                    term = jnp.where(who == m, piece, 0.0)
                    sums[m] = term if p == 0 else sums[m] + term
            for m in range(IMAGES):
                zsend[a, zt, m] = sums[m].astype(jnp.bfloat16)

            @pl.when(zt != zz)
            def _():
                z_copy(a, (zt + Z - zz) % Z).start()

    def f_copy(a, d):
        to = (g + d) % G
        return remote(
            fsend.at[a, to], grads_ref.at[a, g], f_send.at[a, d - 1], f_recv.at[a, d - 1], (to, s)
        )

    def sum_z(j):
        a = j // C
        for d in range(1, Z):
            z_copy(a, d).wait_recv()
        total = zsend[a, zz].astype(jnp.float32)
        for d in range(1, Z):
            total += zrecv[a, d - 1].astype(jnp.float32)
        total = total.astype(jnp.bfloat16)
        for m in range(IMAGES):
            for i in range(GPI):
                fsend[a, m * GPI + i] = total[m, i]
        grads_ref[a, g] = fsend[a, g]
        for d in range(1, G):
            f_copy(a, d).start()

    @pl.loop(0, KVH + 4)
    def _(j):
        @pl.when(j < KVH)
        def _():
            @pl.when(j + 3 < KVH)
            def _():
                y_forward(j + 3)

            @pl.when(j + 2 < KVH)
            def _():
                xz_forward(j + 2)

            @pl.when(j + 1 < KVH)
            def _():
                last_forward(j + 1)

            @pl.when(j + 5 < KVH)
            def _():
                issue(j + 5)

            sib_copy(j).wait_recv()
            for d in range(1, C):
                fwd_all(j, d).wait_recv()
            compute(j)
            start_pieces(j)

        @pl.when(j == 1)
        def _():
            for i in range(len(peers)):
                id_copy(i).wait()

        @pl.when((j >= 2) & (j < KVH + 2) & (owner((j + KVH - 2) % KVH, kind) == g))
        def _():
            sum_images(j - 2)

        @pl.when((j >= 4) & (owner((j + KVH - 4) % KVH, kind) == g))
        def _():
            sum_z(j - 4)

    @pl.loop(0, KVH // C)
    def _(a):
        for d in range(1, G):
            f_copy(a, d).wait()
        for d in range(1, Z):
            z_copy(a, d).wait_send()

    @pl.loop(0, KVH)
    def _(j):
        sib_copy(j).wait_send()
        for d in range(1, C):
            for each in (y_copy, x_copy, z1_copy, xz_copy, zx_copy, fwd_all):
                each(j, d).wait_send()
        wait_sent_pieces(j)


def per_device(queries, image_keys, image_values, gate_logit, block_image, image_counts, output_grad):
    G, S = lax.axis_size("grp"), lax.axis_size("seq")
    C, Z, GPI = G // 2, S // 2, G // IMAGES
    rows = queries.shape[0]
    assert rows == BLK and 2 * KVH % G == 0
    A = KVH // C
    rr = SLOT // (GPI * S)
    eighth = image_keys.shape[0] // 8
    smem = pl.BlockSpec(memory_space=pltpu.SMEM)
    vmem = pl.BlockSpec(memory_space=pltpu.VMEM)
    hbm = pl.BlockSpec(memory_space=pltpu.HBM)
    dma = pltpu.SemaphoreType.DMA
    bf16 = jnp.bfloat16
    attended, query_grad, grads = pl.pallas_call(
        functools.partial(kernel, G, S),
        in_specs=[smem] * 3 + [hbm] * 4,
        out_specs=[vmem] * 3,
        out_shape=[
            jax.ShapeDtypeStruct(queries.shape, bf16),
            jax.ShapeDtypeStruct(queries.shape, bf16),
            jax.ShapeDtypeStruct((A, G, rr, DH), bf16),
        ],
        scratch_shapes=[
            pltpu.VMEM(queries.shape, bf16),
            pltpu.VMEM(queries.shape, bf16),
            pltpu.VMEM(image_keys.shape, bf16),
            pltpu.VMEM(image_keys.shape, bf16),
            dma((4,)),
            pltpu.VMEM((KVH, G, 2, 2, 2, 2, eighth, DH), bf16),
            pltpu.VMEM((2 * G, 8, DH), jnp.int32),
            pltpu.VMEM((KVH, 2, 2, GPI, Z, rr, DH), bf16),
            pltpu.VMEM((A, 2 * G, GPI, Z, rr, DH), bf16),
            pltpu.VMEM((A, Z, IMAGES, GPI, rr, DH), bf16),
            pltpu.VMEM((A, Z - 1, IMAGES, GPI, rr, DH), bf16),
            pltpu.VMEM((A, G, rr, DH), bf16),
            dma((2 * G - 1,)), dma((2 * G - 1,)),
            dma((KVH,)), dma((KVH,)),
        ]
        + [dma((KVH, C - 1))] * 12
        + [
            dma((KVH, 2, 2)), dma((A, 2 * G)),
            dma((A, Z - 1)), dma((A, Z - 1)),
            dma((A, G - 1)), dma((A, G - 1)),
        ],
        compiler_params=pltpu.CompilerParams(
            collective_id=0, has_side_effects=True, vmem_limit_bytes=48 << 20
        ),
        cost_estimate=pl.CostEstimate(
            flops=12 * rows * KVH * GROUPS * SLOT * DH,
            bytes_accessed=16 << 20,
            transcendentals=rows * KVH * GROUPS * SLOT,
        ),
    )(block_image, image_counts, gate_logit, queries, output_grad, image_keys, image_values)
    grads = grads.reshape(A, 2, C // 2, 2, rr, DH).transpose(1, 4, 0, 2, 3, 5)
    grads = grads.reshape(2, rr, KVH * DH)
    return attended, query_grad, grads[0], grads[1]


def solution(mesh):
    rows = P(("grp", "seq"), None)
    return jax.shard_map(
        per_device,
        mesh=mesh,
        in_specs=(rows, P("grp", None), P("grp", None), P(), P("grp", None), P(), rows),
        out_specs=(rows, rows, rows, rows),
        check_vma=False,
    )
```
